32 devices in a mesh: job: 2 (over y), seg: 4 (over x, core), blk: 4 (over z).
Axes of the slice: x: 2, y: 2, z: 4, core: 2. Of those that a mesh axis runs over, the one named last changes fastest.
Arguments:
- amplitudes: float32 [8, 16, 128, 128], P(('job', 'seg'), 'blk'), parts along dimension 0, may hold values from -11 to 11, as said below
- left_env: float32 [8, 16, 128, 128], P(('job', 'seg'), 'blk'), parts along dimension 0, may hold values from -2 to 6, as said below
- right_env: float32 [8, 16, 128, 128], P(('job', 'seg'), 'blk'), parts along dimension 0, may hold values from -2 to 6, as said below
- hop_left: bfloat16 [8, 16, 12, 128, 128], P(('job', 'seg'), 'blk'), parts along dimension 0, may hold values from -0.5 to 0.5
- hop_right: bfloat16 [8, 16, 12, 128, 128], P(('job', 'seg'), 'blk'), parts along dimension 0, may hold values from -0.5 to 0.5
- charges: int32 [32, 2], P('job'), parts along dimension 0, may hold values from -6 to 6
- block_dims: int32 [32, 2], P(('job', 'blk')), parts along dimension 0, may hold values from 64 to 128, as said below
- kept_states: int32 [32], P(('job', 'blk')), parts along dimension 0, may hold values from 32 to 64
- fetch_table: int32 [8, 4, 2], P('job'), parts along dimension 0, may hold values from -1 to 3, as said below
- term_slots: int32 [32, 12], P(('job', 'blk')), parts along dimension 0, may hold values from 0 to 7, as said below
Outputs:
- wave: float32 [8, 16, 128, 128], P(('job', 'seg'), 'blk'), parts along dimension 0
- boundary_env: float32 [8, 16, 128, 128], P(('job', 'seg'), 'blk'), parts along dimension 0
- energies: float32 [8, 2], P(('job', 'seg')), parts along dimension 0
The draws below stay inside these ranges and needn't reach their ends.
There are 2 independent parts, one for each index of `job`. The reference program is written for one: setup_inputs(seed, part) draws one part's arguments, and reference() takes and returns one part's arrays. A program takes and returns all parts, laid end to end along the dimension named above; each array names one. Nothing has to cross between parts.
Inputs may be any that keep to these rules, and one draw needn't show every extreme that they name: `amplitudes`: values of either sign, scaled by a factor per block that differs between blocks, and in some draws also by a factor per row. `left_env`: each block is symmetric. `right_env`: each block is symmetric. `block_dims`: some block has 128 live rows and some block 128 live columns. fetch_table[e, d, c] is the index, within device d's 4 blocks, of the block that fills slot d * 2 + c of device e, and -1 exactly where no hopping term of device e names that slot; the slots of one source device name different blocks; on every device both slots of some source device are named. term_slots[b, k] names a slot of the device that holds block b (blocks b with equal b // 4); the slot's source device is the slot // 2.
All inputs are finite; a program needn't handle non-finite values.
Results may differ from the reference program's by a relative error of at most 0.005.
Values may be sent and summed in bfloat16 or wider, within the bound.
A program may use at most 64 MiB of HBM per device.

```python
import jax
import jax.numpy as jnp
from jax import lax

BDIM = 128
NHOP = 12
BLK_DEV = 4
CAP = 2
ITERS = 2
NBLOCKS = 16
SEGS = 4
N_BLK = 4


def symmetric_blocks(key, diag_low, diag_high):
    diag_key, noise_key = jax.random.split(key)
    diagonal = jax.random.uniform(diag_key, (SEGS, NBLOCKS, BDIM), jnp.float32, diag_low, diag_high)
    noise = jnp.clip(jax.random.normal(noise_key, (SEGS, NBLOCKS, BDIM, BDIM), jnp.float32), -4.0, 4.0)
    mirrored = (noise + jnp.swapaxes(noise, 2, 3)) * (0.7 / jnp.sqrt(jnp.float32(BDIM)))
    positions = jnp.arange(BDIM)
    on_diagonal = positions[:, None] == positions[None, :]
    return jnp.where(on_diagonal[None, None], diagonal[:, :, :, None], jnp.clip(mirrored, -2.0, 2.0))


def draw_left_env(key, part):
    key = jax.random.fold_in(key, 21)
    return symmetric_blocks(key, 1.0, 4.0)


def draw_right_env(key, part):
    key = jax.random.fold_in(key, 22)
    return symmetric_blocks(key, 1.0, 4.0)


def draw_amplitudes(key, part):
    key = jax.random.fold_in(key, 31)
    value_key = jax.random.fold_in(key, 0)
    ramp = 0.6 + 1.2 * jnp.arange(NBLOCKS, dtype=jnp.float32) / max(NBLOCKS - 1, 1)
    values = jax.random.normal(value_key, (SEGS, NBLOCKS, BDIM, BDIM), jnp.float32)
    return jnp.clip(values, -6.0, 6.0) * ramp[None, :, None, None]


def draw_block_dims(key, part):
    key = jax.random.fold_in(key, 11)
    dims_key, chosen_key = jax.random.split(key)
    drawn_dims = jax.random.randint(dims_key, (NBLOCKS, 2), BDIM // 2, BDIM + 1)
    chosen = jax.random.randint(chosen_key, (2,), 0, NBLOCKS)
    rows_hit = jnp.arange(NBLOCKS)[:, None] == chosen[None, :]
    return jnp.where(rows_hit, BDIM, drawn_dims).astype(jnp.int32)


def routing_tables(key):
    slot_key, source_key, order_key, first_key, second_key = jax.random.split(key, 5)
    hop_count = BLK_DEV * NHOP
    slot_count = N_BLK * CAP
    picks = jax.random.randint(slot_key, (N_BLK, hop_count), 0, slot_count)
    source = jax.random.randint(source_key, (N_BLK,), 0, N_BLK)
    column = jnp.arange(hop_count)[None, :]
    picks = jnp.where(column == 0, source[:, None] * CAP, jnp.where(column == 1, source[:, None] * CAP + 1, picks))
    picks = jax.random.permutation(order_key, picks, axis=1, independent=True)
    used = jnp.any(picks[:, :, None] == jnp.arange(slot_count)[None, None, :], axis=1)
    first_pick = jax.random.randint(first_key, (N_BLK, N_BLK), 0, BLK_DEV)
    second_pick = (first_pick + 1 + jax.random.randint(second_key, (N_BLK, N_BLK), 0, BLK_DEV - 1)) % BLK_DEV
    table = jnp.stack([first_pick, second_pick], axis=2)
    table = jnp.where(used.reshape(N_BLK, N_BLK, CAP), table, -1)
    return (picks.reshape(NBLOCKS, NHOP).astype(jnp.int32), table.astype(jnp.int32))


def draw_term_slots(key, part):
    return routing_tables(key)[0]


def draw_fetch_table(key, part):
    return routing_tables(key)[1]


def place_ends(values, stream_key, least, largest):
    extent = values.shape
    place = [jax.random.randint(jax.random.fold_in(stream_key, axis), (), 0, extent[axis]) for axis in range(len(extent))]
    values = values.at[tuple(place)].set(least)
    longest = extent.index(max(extent))
    place[longest] = (place[longest] + 1) % extent[longest]
    return values.at[tuple(place)].set(largest)


def steps_of(stream_key, shape, shards, smallest, top_value):
    def one(dim, parts):
        draws = jax.random.uniform(jax.random.fold_in(jax.random.fold_in(stream_key, 6), dim), (parts,), jnp.float32, smallest / len(shards), top_value / len(shards))
        return jnp.repeat(jnp.exp(draws), shape[dim] // parts).reshape((-1,) + (1,) * (len(shape) - dim - 1))

    level = one(*shards[0])
    for cut in shards[1:]:
        level = level * one(*cut)
    return level


def scatter_about(rng, shape, deviation, bound, cuts=(), held_as=jnp.bfloat16):
    gain = steps_of(rng, shape, cuts, -0.22, 0.18) if cuts else 1.0
    drawn = jax.random.normal(rng, shape, jnp.float32) * deviation * gain
    return jnp.minimum(jnp.maximum(drawn, -bound), bound).astype(held_as)


def setup_inputs(seed: int = 0, part: int = 0) -> dict:
    keys = jax.random.split(jax.random.key(seed), 11)
    part_splits = jax.random.split(jax.random.fold_in(keys[10], part), 11)
    return {
        "amplitudes": draw_amplitudes(jax.random.fold_in(jax.random.fold_in(keys[10], part), 71), part),
        "left_env": draw_left_env(jax.random.fold_in(jax.random.fold_in(keys[10], part), 71), part),
        "right_env": draw_right_env(jax.random.fold_in(jax.random.fold_in(keys[10], part), 71), part),
        "hop_left": scatter_about(part_splits[3], (SEGS, NBLOCKS, NHOP, BDIM, BDIM), BDIM ** -0.5, 0.5, ((0, 4), (1, 4))),
        "hop_right": scatter_about(part_splits[4], (SEGS, NBLOCKS, NHOP, BDIM, BDIM), BDIM ** -0.5, 0.5, ((0, 4), (1, 4))),
        "charges": place_ends(jax.random.randint(part_splits[5], (NBLOCKS, 2), -6, 7), jax.random.fold_in(part_splits[5], 1), -6, 6).astype(jnp.int32),
        "block_dims": draw_block_dims(jax.random.fold_in(jax.random.fold_in(keys[10], part), 71), part),
        "kept_states": place_ends(jax.random.randint(part_splits[7], (NBLOCKS,), BDIM // 4, BDIM // 2 + 1), jax.random.fold_in(part_splits[7], 1), BDIM // 4, (BDIM // 2 + 1) - 1).astype(jnp.int32),
        "fetch_table": draw_fetch_table(jax.random.fold_in(jax.random.fold_in(keys[10], part), 71), part),
        "term_slots": draw_term_slots(jax.random.fold_in(jax.random.fold_in(keys[10], part), 71), part),
    }


STEP_SIZE = 0.5
ZEEMAN = 0.5
EPSILON = 1e-06
HIGHEST = lax.Precision.HIGHEST

def partner_index(fetch_table, term_slots):
    owners = jnp.arange(NBLOCKS, dtype=jnp.int32) // BLK_DEV
    source = term_slots // CAP
    within = term_slots % CAP
    local_pick = fetch_table[owners[:, None], source, within]
    return (source * BLK_DEV + local_pick).astype(jnp.int32)

def hop_image(amp_half, hop_left, hop_right, partner, parity):
    gathered = amp_half[partner].astype(jnp.float32)
    inner = jnp.einsum('bkij,bkjl->bkil', hop_left.astype(jnp.float32), gathered, precision=HIGHEST).astype(jnp.bfloat16)
    outer = jnp.einsum('bkij,bkjl->bkil', inner.astype(jnp.float32), hop_right.astype(jnp.float32), precision=HIGHEST)
    return lax.optimization_barrier(jnp.sum(outer * parity[:, :, None, None], axis=1))

def apply_ham(amplitudes, left_one, right_one, hop_l, hop_r, partner, parity, zeeman_term, live_mask):
    amp_half = amplitudes.astype(jnp.bfloat16)
    local_part = jnp.einsum('bij,bjl->bil', left_one, amplitudes, precision=HIGHEST)
    local_part = local_part + jnp.einsum('bij,bjl->bil', amplitudes, right_one, precision=HIGHEST)
    return live_mask * (local_part + zeeman_term * amplitudes + hop_image(amp_half, hop_l, hop_r, partner, parity))

def davidson(start, left_one, right_one, hop_l, hop_r, partner, parity, zeeman_term, live_mask):
    entries = float(NBLOCKS * BDIM * BDIM)
    diag_sum = jnp.diagonal(left_one, axis1=1, axis2=2)[:, :, None] + jnp.diagonal(right_one, axis1=1, axis2=2)[:, None, :] + zeeman_term
    amplitudes = live_mask * start
    norm_sq = jnp.sum(amplitudes * amplitudes)
    amplitudes = amplitudes * lax.rsqrt(norm_sq / entries + EPSILON)
    energy = jnp.float32(0.0)
    for iteration in range(ITERS):
        image = apply_ham(amplitudes, left_one, right_one, hop_l, hop_r, partner, parity, zeeman_term, live_mask)
        energy = jnp.sum(amplitudes * image) / entries
        correction = live_mask * (image - energy * amplitudes) / (1.0 + jnp.abs(diag_sum - energy))
        trial = amplitudes - STEP_SIZE * correction
        norm_sq = jnp.sum(trial * trial)
        amplitudes = trial * lax.rsqrt(norm_sq / entries + EPSILON)
    return (amplitudes, energy)

def boundary_of(amplitudes, left_one, kept_states):
    column = jnp.arange(BDIM, dtype=jnp.int32)
    kept_mask = (column[None, None, :] < kept_states[:, None, None]).astype(jnp.float32)
    truncated = amplitudes * kept_mask
    carried = jnp.einsum('bij,bjl->bil', left_one, truncated, precision=HIGHEST)
    return jnp.einsum('bji,bjl->bil', truncated, carried, precision=HIGHEST) / BDIM

def reference(amplitudes, left_env, right_env, hop_left, hop_right, charges, block_dims, kept_states, fetch_table, term_slots):
    partner = partner_index(fetch_table, term_slots)
    parity = (1 - 2 * jnp.remainder(charges[partner, 0], 2)).astype(jnp.float32)
    positions = jnp.arange(BDIM, dtype=jnp.int32)
    live_mask = ((positions[None, :, None] < block_dims[:, 0, None, None]) & (positions[None, None, :] < block_dims[:, 1, None, None])).astype(jnp.float32)
    zeeman_term = (ZEEMAN * charges[:, 1].astype(jnp.float32))[:, None, None]

    def first_update(operands):
        start, left_one, right_one, hop_l, hop_r = operands
        result, energy = davidson(start, left_one, right_one, hop_l, hop_r, partner, parity, zeeman_term, live_mask)
        return (result, energy, boundary_of(result, left_one, kept_states))
    updated, first_energy, outgoing = lax.map(first_update, (amplitudes, left_env, right_env, hop_left, hop_right))
    incoming = jnp.concatenate([jnp.zeros_like(outgoing[:1]), outgoing[:-1]], axis=0)

    def second_update(operands):
        start, left_one, right_one, hop_l, hop_r = operands
        return davidson(start, left_one, right_one, hop_l, hop_r, partner, parity, zeeman_term, live_mask)
    final_wave, second_energy = lax.map(second_update, (updated, left_env + incoming, right_env, hop_left, hop_right))
    return (final_wave, outgoing, jnp.stack([first_energy, second_energy], axis=1))
```

```python
import functools

import jax
import jax.numpy as jnp
from jax import lax
from jax.experimental import pallas as pl
from jax.experimental.pallas import tpu as pltpu
from jax.sharding import PartitionSpec as P

ITERS = 2
STEP_SIZE = 0.5
ZEEMAN = 0.5
EPSILON = 1e-06
MESH = pl.DeviceIdType.MESH
F32 = jnp.float32
BF16 = jnp.bfloat16


def mm(a, b):
    return jnp.dot(a, b, preferred_element_type=F32)


def tile_sum(values):
    rows, cols = values.shape
    return jnp.sum(values.reshape(rows // 8, 8, cols), axis=0)


def split(values):
    high = values.astype(BF16)
    return high, (values - high.astype(F32)).astype(BF16)


def kernel(
    n, segs, nb, dim, nhop, cap,
    amp_hbm, left_hbm, right_hbm, hopl_hbm, hopr_hbm,
    charges, dims, kept, fetch, slots,
    wave_hbm, bound_hbm, energy_ref,
    t_v, left_v, right_v, hopl_v, hopr_v,
    signed, send, recv, lmat, rmat, tcol, trow, inner, local, field_diag, mask_v,
    parts, inc_v, inc_send, bound_v,
    in_sem, send_sem, recv_sem, psend_sem, precv_sem, isend_sem, irecv_sem, out_sem,
):
    me = lax.axis_index("blk")
    seg = lax.axis_index("seg")
    seg_next = lax.rem(seg + 1, segs)
    seg_prev = lax.rem(seg + segs - 1, segs)
    peers = [lax.rem(me + d, n) for d in range(1, n)]
    order = sorted(range(n - 1), key=lambda i: -min(i + 1, n - 1 - i))
    entries = float(n * nb * dim * dim)

    loads = [
        pltpu.make_async_copy(src.at[0], dst, in_sem.at[i])
        for i, (src, dst) in enumerate(
            [(amp_hbm, t_v), (left_hbm, left_v), (right_hbm, right_v), (hopl_hbm, hopl_v), (hopr_hbm, hopr_v)]
        )
    ]
    for load in loads:
        load.start()

    barrier = pltpu.get_barrier_semaphore()
    for peer in peers:
        pl.semaphore_signal(barrier, inc=1, device_id={"blk": peer}, device_id_type=MESH)
    pl.semaphore_signal(barrier, inc=1, device_id={"seg": seg_next}, device_id_type=MESH)
    pl.semaphore_signal(barrier, inc=1, device_id={"seg": seg_prev}, device_id_type=MESH)

    row_at = lax.broadcasted_iota(jnp.int32, (dim, dim), 0)
    col_at = lax.broadcasted_iota(jnp.int32, (dim, dim), 1)
    signs = [(1 - 2 * (charges[me * nb + b, 0] & 1)).astype(F32) for b in range(nb)]
    fields = [ZEEMAN * charges[me * nb + b, 1].astype(F32) for b in range(nb)]

    def block_copy(i):
        return pltpu.make_async_remote_copy(
            src_ref=send.at[pl.ds(i * cap, cap)],
            dst_ref=recv.at[pl.ds(me * cap, cap)],
            send_sem=send_sem.at[i],
            recv_sem=recv_sem.at[i],
            device_id={"blk": peers[i]},
            device_id_type=MESH,
        )

    def part_copy(turn, i):
        return pltpu.make_async_remote_copy(
            src_ref=parts.at[turn, me],
            dst_ref=parts.at[turn, me],
            send_sem=psend_sem.at[turn, i],
            recv_sem=precv_sem.at[turn, i],
            device_id={"blk": peers[i]},
            device_id_type=MESH,
        )

    def send_blocks():
        for i in order:
            for c in range(cap):
                send[i * cap + c] = signed[jnp.maximum(fetch[peers[i], me, c], 0)]
            block_copy(i).start()
        for c in range(cap):
            recv[me * cap + c] = signed[jnp.maximum(fetch[me, me, c], 0)]

    def wait_blocks():
        for i in range(n - 1):
            block_copy(i).wait()

    def send_parts(turn, squares, products):
        parts[turn, me] = jnp.concatenate([squares, products], axis=0)
        for i in order:
            part_copy(turn, i).start()

    def wait_parts(turn):
        for i in range(n - 1):
            part_copy(turn, i).wait()
        total = parts[turn, 0]
        for i in range(1, n):
            total = total + parts[turn, i]
        square = jnp.sum(total[0:8], axis=(0, 1), keepdims=True) / entries
        product = jnp.sum(total[8:16], axis=(0, 1), keepdims=True) / entries
        return square, product

    def split_t():
        for b in range(nb):
            high, low = split(t_v[b])
            tcol[b, 0:dim] = high
            tcol[b, dim:2 * dim] = high
            tcol[b, 2 * dim:3 * dim] = low
            trow[b, :, 0:dim] = high
            trow[b, :, dim:2 * dim] = high
            trow[b, :, 2 * dim:3 * dim] = low

    def set_left(b, value):
        high, low = split(value)
        lmat[b, :, 0:dim] = high
        lmat[b, :, dim:2 * dim] = low
        lmat[b, :, 2 * dim:3 * dim] = high

    def diag_column(value):
        return jnp.sum(jnp.where(row_at == col_at, value, 0.0), axis=1, keepdims=True)

    def diag_row(value):
        return jnp.sum(jnp.where(row_at == col_at, value, 0.0), axis=0, keepdims=True)

    def hopping():
        products = jnp.zeros((8, dim), F32)
        for b in range(nb):
            for k in range(nhop):
                inner[b, :, k * dim:(k + 1) * dim] = mm(hopl_v[b, k], recv[slots[b, k]]).astype(BF16)
            image = local[b] + mm(inner[b], hopr_v[b].reshape(nhop * dim, dim))
            local[b] = image
            products = products + tile_sum(t_v[b] * image)
        return products

    def step(energy, scale):
        squares = jnp.zeros((8, dim), F32)
        for b in range(nb):
            old = t_v[b]
            change = mask_v[b] * (local[b] - energy * old) / (1.0 + jnp.abs(field_diag[b] - energy))
            new = scale * (old - STEP_SIZE * change)
            t_v[b] = new
            signed[b] = (new * signs[b]).astype(BF16)
            squares = squares + tile_sum(new * new)
        return squares

    squares = jnp.zeros((8, dim), F32)
    loads[0].wait()
    for b in range(nb):
        live = jnp.where((row_at < dims[b, 0]) & (col_at < dims[b, 1]), 1.0, 0.0)
        mask_v[b] = live
        new = live * t_v[b]
        t_v[b] = new
        signed[b] = (new * signs[b]).astype(BF16)
        squares = squares + tile_sum(new * new)
    pl.semaphore_wait(barrier, n + 1)

    zeros = jnp.zeros((8, dim), F32)
    turn = 0
    energies = []
    for update in range(2):
        for iteration in range(ITERS):
            send_blocks()
            if update == 1 and iteration == 0:
                send_parts(turn, squares, zeros)
            split_t()
            if update == 0 and iteration == 0:
                loads[1].wait()
                loads[2].wait()
                for b in range(nb):
                    set_left(b, left_v[b])
                    high, low = split(right_v[b])
                    rmat[b, 0:dim] = high
                    rmat[b, dim:2 * dim] = low
                    rmat[b, 2 * dim:3 * dim] = high
                    field_diag[b] = diag_column(left_v[b]) + diag_row(right_v[b]) + fields[b]
            if update == 1 and iteration == 0:
                for b in range(nb):
                    from_left = mm(lmat[b], tcol[b])
                    local[b] = from_left + mm(trow[b], rmat[b]) + fields[b] * t_v[b]
                    high, low = split(from_left)
                    bound_v[b] = lax.dot_general(
                        tcol[b],
                        jnp.concatenate([high, low, high], axis=0),
                        (((0,), (0,)), ((), ())),
                        preferred_element_type=F32,
                    )
                square, _ = wait_parts(turn)
                turn = 1 - turn
                scale = lax.rsqrt(square + EPSILON)
                for b in range(nb):
                    keep = (row_at < kept[b]) & (col_at < kept[b])
                    outgoing = jnp.where(keep, bound_v[b] * (scale * scale * (1.0 / dim)), 0.0)
                    bound_v[b] = outgoing
                    inc_send[b] = outgoing.astype(BF16)
                inc_copy = pltpu.make_async_remote_copy(
                    src_ref=inc_send,
                    dst_ref=inc_v,
                    send_sem=isend_sem,
                    recv_sem=irecv_sem,
                    device_id={"seg": seg_next},
                    device_id_type=MESH,
                )
                inc_copy.start()
                bound_out = pltpu.make_async_copy(bound_v, bound_hbm.at[0], out_sem.at[0])
                bound_out.start()
                inc_copy.wait()
                for b in range(nb):
                    incoming = jnp.where(seg > 0, inc_v[b], jnp.zeros((dim, dim), BF16))
                    wide = incoming.astype(F32)
                    local[b] = local[b] + mm(
                        jnp.concatenate([incoming, incoming], axis=1), tcol[b, dim:3 * dim]
                    )
                    set_left(b, left_v[b] + wide)
                    field_diag[b] = field_diag[b] + diag_column(wide)
            else:
                for b in range(nb):
                    local[b] = mm(lmat[b], tcol[b]) + mm(trow[b], rmat[b]) + fields[b] * t_v[b]
            if update == 0 and iteration == 0:
                loads[3].wait()
                loads[4].wait()
            wait_blocks()
            products = hopping()
            send_parts(turn, squares, products)
            square, product = wait_parts(turn)
            turn = 1 - turn
            scale = lax.rsqrt(square + EPSILON)
            if update == 1 and iteration == 0:
                scale = scale * lax.rsqrt(square * scale * scale + EPSILON)
            energy = product * scale * scale
            squares = step(energy, scale)
        energies.append(energy)

    send_parts(turn, squares, zeros)
    which = lax.broadcasted_iota(jnp.int32, (1, 2), 1)
    energy_ref[...] = jnp.where(which == 0, energies[0], energies[1])
    square, _ = wait_parts(turn)
    scale = lax.rsqrt(square + EPSILON)
    for b in range(nb):
        t_v[b] = t_v[b] * scale
    wave_out = pltpu.make_async_copy(t_v, wave_hbm.at[0], out_sem.at[1])
    wave_out.start()
    bound_out.wait()
    wave_out.wait()


def on_device(n, segs, *args):
    amplitudes, left_env, right_env, hop_left, hop_right, charges, dims, kept, fetch, slots = args
    nb, dim = amplitudes.shape[1], amplitudes.shape[2]
    nhop = hop_left.shape[2]
    cap = fetch.shape[2]
    any_space = pl.BlockSpec(memory_space=pl.ANY)
    smem = pl.BlockSpec(memory_space=pltpu.SMEM)
    vmem = pl.BlockSpec(memory_space=pltpu.VMEM)
    blocks = (nb, dim, dim)
    dma = pltpu.SemaphoreType.DMA
    scratch = [
        pltpu.VMEM(blocks, F32),
        pltpu.VMEM(blocks, F32),
        pltpu.VMEM(blocks, F32),
        pltpu.VMEM((nb, nhop, dim, dim), BF16),
        pltpu.VMEM((nb, nhop, dim, dim), BF16),
        pltpu.VMEM(blocks, BF16),
        pltpu.VMEM(((n - 1) * cap, dim, dim), BF16),
        pltpu.VMEM((n * cap, dim, dim), BF16),
        pltpu.VMEM((nb, dim, 3 * dim), BF16),
        pltpu.VMEM((nb, 3 * dim, dim), BF16),
        pltpu.VMEM((nb, 3 * dim, dim), BF16),
        pltpu.VMEM((nb, dim, 3 * dim), BF16),
        pltpu.VMEM((nb, dim, nhop * dim), BF16),
        pltpu.VMEM(blocks, F32),
        pltpu.VMEM(blocks, F32),
        pltpu.VMEM(blocks, F32),
        pltpu.VMEM((2, n, 16, dim), F32),
        pltpu.VMEM(blocks, BF16),
        pltpu.VMEM(blocks, BF16),
        pltpu.VMEM(blocks, F32),
        dma((5,)),
        dma((n - 1,)),
        dma((n - 1,)),
        dma((2, n - 1)),
        dma((2, n - 1)),
        dma,
        dma,
        dma((2,)),
    ]
    return pl.pallas_call(
        functools.partial(kernel, n, segs, nb, dim, nhop, cap),
        out_shape=(
            jax.ShapeDtypeStruct(amplitudes.shape, F32),
            jax.ShapeDtypeStruct(amplitudes.shape, F32),
            jax.ShapeDtypeStruct((1, 2), F32),
        ),
        in_specs=[any_space] * 5 + [smem] * 5,
        out_specs=(any_space, any_space, vmem),
        scratch_shapes=scratch,
        compiler_params=pltpu.CompilerParams(
            collective_id=0, has_side_effects=True, vmem_limit_bytes=40 * 1024 * 1024
        ),
    )(amplitudes, left_env, right_env, hop_left, hop_right, charges, dims, kept, fetch, slots)


def solution(mesh):
    placed = (
        P(("job", "seg"), "blk", None, None),
        P(("job", "seg"), "blk", None, None),
        P(("job", "seg"), "blk", None, None),
        P(("job", "seg"), "blk", None, None, None),
        P(("job", "seg"), "blk", None, None, None),
        P("job", None),
        P(("job", "blk"), None),
        P(("job", "blk")),
        P("job", None, None),
        P(("job", "blk"), None),
    )
    return jax.shard_map(
        functools.partial(on_device, mesh.shape["blk"], mesh.shape["seg"]),
        mesh=mesh,
        in_specs=placed,
        out_specs=(
            P(("job", "seg"), "blk", None, None),
            P(("job", "seg"), "blk", None, None),
            P(("job", "seg"), None),
        ),
        check_vma=False,
    )
```

```python
import functools

import jax
import jax.numpy as jnp
from jax import lax
from jax.experimental import pallas as pl
from jax.experimental.pallas import tpu as pltpu
from jax.sharding import PartitionSpec as P

ITERS = 2
STEP_SIZE = 0.5
ZEEMAN = 0.5
EPSILON = 1e-06
MESH = pl.DeviceIdType.MESH
F32 = jnp.float32
BF16 = jnp.bfloat16


def mm(a, b):
    return jnp.dot(a, b, preferred_element_type=F32)


def tile_sum(values):
    rows, cols = values.shape
    return jnp.sum(values.reshape(rows // 8, 8, cols), axis=0)


def split(values):
    high = values.astype(BF16)
    return high, (values - high.astype(F32)).astype(BF16)


def each(count, body):
    if count <= 16:
        for index in range(count):
            body(index)
    else:
        lax.fori_loop(0, count, lambda index, _: (body(index), 0)[1], 0)


def kernel(
    n, segs, nb, dim, nhop, cap,
    amp_hbm, left_hbm, right_hbm, hopl_hbm, hopr_hbm,
    charges, dims, kept, fetch, slots,
    wave_hbm, bound_hbm, energy_ref,
    t_v, left_v, right_v, hopl_v, hopr_v,
    signed, send, recv, lmat, rmat, tcol, trow, inner, local, diag_v, mask_v,
    parts, inc_v, inc_send, bound_v,
    copy_v, slot_t, slot_x, slot_diag, vec_v, vec_send, vec_recv, norm_send, norm_recv,
    in_sem, send_sem, recv_sem, psend_sem, precv_sem, isend_sem, irecv_sem, out_sem,
    vsend_sem, vrecv_sem, nsend_sem, nrecv_sem,
):
    me = lax.axis_index("blk")
    seg = lax.axis_index("seg")
    seg_next = lax.rem(seg + 1, segs)
    seg_prev = lax.rem(seg + segs - 1, segs)
    peers = [lax.rem(me + d, n) for d in range(1, n)]
    group = [lax.rem(me + d, n) for d in range(n)]
    order = sorted(range(n - 1), key=lambda i: -min(i + 1, n - 1 - i))
    entries = float(n * nb * dim * dim)

    loads = [
        pltpu.make_async_copy(src.at[0], dst, in_sem.at[i])
        for i, (src, dst) in enumerate(
            [(amp_hbm, t_v), (left_hbm, left_v), (right_hbm, right_v), (hopl_hbm, hopl_v), (hopr_hbm, hopr_v)]
        )
    ]
    for load in loads:
        load.start()

    barrier = pltpu.get_barrier_semaphore()
    for peer in peers:
        pl.semaphore_signal(barrier, inc=1, device_id={"blk": peer}, device_id_type=MESH)
    for peer in group:
        for other in (seg_next, seg_prev):
            pl.semaphore_signal(barrier, inc=1, device_id={"seg": other, "blk": peer}, device_id_type=MESH)

    row_at = lax.broadcasted_iota(jnp.int32, (dim, dim), 0)
    col_at = lax.broadcasted_iota(jnp.int32, (dim, dim), 1)
    signs = [(1 - 2 * (charges[0, me * nb + b] & 1)).astype(F32) for b in range(nb)]
    fields = [ZEEMAN * charges[1, me * nb + b].astype(F32) for b in range(nb)]

    def block_copy(half, i):
        return pltpu.make_async_remote_copy(
            src_ref=send.at[pl.ds(i * cap, cap)],
            dst_ref=recv.at[half, pl.ds(me * cap, cap)],
            send_sem=send_sem.at[half, i],
            recv_sem=recv_sem.at[half, i],
            device_id={"blk": peers[i]},
            device_id_type=MESH,
        )

    def part_copy(turn, i):
        return pltpu.make_async_remote_copy(
            src_ref=parts.at[turn, me],
            dst_ref=parts.at[turn, me],
            send_sem=psend_sem.at[turn, i],
            recv_sem=precv_sem.at[turn, i],
            device_id={"blk": peers[i]},
            device_id_type=MESH,
        )

    def vec_copy(i):
        return pltpu.make_async_remote_copy(
            src_ref=vec_send.at[pl.ds(i * cap, cap)],
            dst_ref=vec_recv.at[pl.ds(me * cap, cap)],
            send_sem=vsend_sem.at[i],
            recv_sem=vrecv_sem.at[i],
            device_id={"blk": peers[i]},
            device_id_type=MESH,
        )

    def norm_copy(i):
        return pltpu.make_async_remote_copy(
            src_ref=norm_send,
            dst_ref=norm_recv.at[me],
            send_sem=nsend_sem.at[i],
            recv_sem=nrecv_sem.at[i],
            device_id={"blk": group[i], "seg": seg_next},
            device_id_type=MESH,
        )

    def picked(device, c):
        return jnp.maximum(fetch[device, c, me], 0)

    def send_blocks(half):
        for i in order:
            for c in range(cap):
                send[i * cap + c] = signed[picked(peers[i], c)]
            block_copy(half, i).start()
        for c in range(cap):
            recv[half, me * cap + c] = signed[picked(me, c)]

    def wait_blocks(half):
        for i in range(n - 1):
            block_copy(half, i).wait()

    def diag_row(value):
        return jnp.sum(jnp.where(row_at == col_at, value, 0.0), axis=0, keepdims=True)

    def diag_of(pair):
        column = jnp.sum(jnp.where(row_at == col_at, pair[0:1], 0.0), axis=1, keepdims=True)
        return column + pair[1:2]

    def send_vecs():
        for i in order:
            for c in range(cap):
                vec_send[i * cap + c] = vec_v[picked(peers[i], c)]
            vec_copy(i).start()
        for c in range(cap):
            vec_recv[me * cap + c] = vec_v[picked(me, c)]

    def wait_vecs():
        for i in range(n - 1):
            vec_copy(i).wait()

        def one(index):
            slot_diag[index] = diag_of(vec_recv[index])

        each(n * cap, one)

    def send_parts(turn, squares, products):
        parts[turn, me] = jnp.concatenate([squares, products], axis=0)
        for i in order:
            part_copy(turn, i).start()

    def total_of(tile):
        return jnp.sum(tile, axis=(0, 1), keepdims=True)

    def wait_parts(turn):
        for i in range(n - 1):
            part_copy(turn, i).wait()
        total = parts[turn, 0]
        for i in range(1, n):
            total = total + parts[turn, i]
        return total_of(total[0:8]) / entries, total_of(total[8:16]) / entries

    def split_t():
        for b in range(nb):
            high, low = split(t_v[b])
            tcol[b, 0:dim] = high
            tcol[b, dim:2 * dim] = high
            tcol[b, 2 * dim:3 * dim] = low
            trow[b, :, 0:dim] = high
            trow[b, :, dim:2 * dim] = high
            trow[b, :, 2 * dim:3 * dim] = low

    def set_left(b, value):
        high, low = split(value)
        lmat[b, :, 0:dim] = high
        lmat[b, :, dim:2 * dim] = low
        lmat[b, :, 2 * dim:3 * dim] = high

    def local_products(with_left):
        for b in range(nb):
            value = mm(trow[b], rmat[b]) + fields[b] * t_v[b]
            if with_left:
                value = value + mm(lmat[b], tcol[b])
            local[b] = value

    def hopping(finish):
        for b in range(nb):
            for k in range(nhop):
                inner[b, :, k * dim:(k + 1) * dim] = mm(hopl_v[b, k], slot_x[slots[b, k]]).astype(BF16)
            local[b] = local[b] + mm(inner[b], hopr_v[b].reshape(nhop * dim, dim))
        finish()
        products = jnp.zeros((8, dim), F32)
        for b in range(nb):
            image = mask_v[b] * local[b]
            local[b] = image
            products = products + tile_sum(t_v[b] * image)
        return products

    def send_image(half, squares, products):
        guess = total_of(products) / (total_of(squares) + 1e-30)
        for b in range(nb):
            behind = signs[b] * t_v[b] - copy_v[b]
            weight = guess + (1.0 / STEP_SIZE) * (1.0 + jnp.abs(diag_v[b] - guess))
            signed[b] = (signs[b] * local[b] - behind * weight).astype(BF16)
        send_blocks(half)

    def advance(old, image, diag, energy, scale):
        change = (image - energy * old) / (1.0 + jnp.abs(diag - energy))
        return scale * (old - STEP_SIZE * change)

    def step(energy, scale):
        squares = jnp.zeros((8, dim), F32)
        for b in range(nb):
            new = advance(t_v[b], local[b], diag_v[b], energy, scale)
            t_v[b] = new
            squares = squares + tile_sum(new * new)
        return squares

    def step_copies(energy, scale):
        for b in range(nb):
            copy_v[b] = advance(copy_v[b], signed[b].astype(F32), diag_v[b], energy, scale)

    def step_slots(half, energy, scale):
        def one(index):
            new = advance(slot_t[index], recv[half, index].astype(F32), slot_diag[index], energy, scale)
            slot_t[index] = new
            slot_x[index] = new.astype(BF16)

        each(n * cap, one)

    def nothing():
        pass

    squares = jnp.zeros((8, dim), F32)
    loads[0].wait()
    for b in range(nb):
        live = jnp.where((row_at < dims[0, b]) & (col_at < dims[1, b]), 1.0, 0.0)
        mask_v[b] = live
        new = live * t_v[b]
        t_v[b] = new
        first = (new * signs[b]).astype(BF16)
        signed[b] = first
        copy_v[b] = first.astype(F32)
        squares = squares + tile_sum(new * new)
    pl.semaphore_wait(barrier, n - 1 + 2 * n)
    send_blocks(0)
    loads[1].wait()
    loads[2].wait()
    for b in range(nb):
        vec_v[b, 0:1] = diag_row(left_v[b]) + fields[b]
        vec_v[b, 1:2] = diag_row(right_v[b])
    send_vecs()
    split_t()
    for b in range(nb):
        set_left(b, left_v[b])
        high, low = split(right_v[b])
        rmat[b, 0:dim] = high
        rmat[b, dim:2 * dim] = low
        rmat[b, 2 * dim:3 * dim] = high
        diag_v[b] = diag_of(vec_v[b])
    local_products(True)
    loads[3].wait()
    loads[4].wait()
    wait_blocks(0)

    def widen(index):
        first = recv[0, index]
        slot_x[index] = first
        slot_t[index] = first.astype(F32)

    each(n * cap, widen)

    products = hopping(nothing)
    send_parts(0, squares, products)
    send_image(1, squares, products)
    wait_vecs()
    square, product = wait_parts(0)
    scale = lax.rsqrt(square + EPSILON)
    energy = product * scale * scale
    squares = step(energy, scale)
    step_copies(energy, scale)
    split_t()
    local_products(True)
    wait_blocks(1)
    step_slots(1, energy, scale)

    products = hopping(nothing)
    send_parts(1, squares, products)
    send_image(0, squares, products)
    square, product = wait_parts(1)
    scale = lax.rsqrt(square + EPSILON)
    energy = product * scale * scale
    first_energy = energy
    squares = step(energy, scale)
    norm_send[...] = squares
    for i in range(n):
        norm_copy(i).start()
    split_t()
    for b in range(nb):
        high, low = split(mm(lmat[b], tcol[b]))
        raw = lax.dot_general(
            tcol[b],
            jnp.concatenate([high, low, high], axis=0),
            (((0,), (0,)), ((), ())),
            preferred_element_type=F32,
        )
        keep = (row_at < kept[b]) & (col_at < kept[b])
        raw = jnp.where(keep, raw, 0.0)
        bound_v[b] = raw
        inc_send[b] = raw.astype(BF16)
    inc_copy = pltpu.make_async_remote_copy(
        src_ref=inc_send,
        dst_ref=inc_v,
        send_sem=isend_sem,
        recv_sem=irecv_sem,
        device_id={"seg": seg_next},
        device_id_type=MESH,
    )
    inc_copy.start()
    step_copies(energy, scale)
    local_products(False)
    wait_blocks(0)
    step_slots(0, energy, scale)

    def add_left():
        for i in range(n):
            norm_copy(i).wait()
        total = norm_recv[0]
        for i in range(1, n):
            total = total + norm_recv[i]
        factor = (1.0 / dim) / (total_of(total) / entries + EPSILON)
        factor = jnp.where(seg > 0, factor, 0.0)
        inc_copy.wait()
        for b in range(nb):
            wide = inc_v[b].astype(F32) * factor
            set_left(b, left_v[b] + wide)
            local[b] = local[b] + mm(lmat[b], tcol[b])
            vec_v[b, 0:1] = vec_v[b, 0:1] + diag_row(wide)
            diag_v[b] = diag_of(vec_v[b])

    products = hopping(add_left)
    send_parts(0, squares, products)
    send_image(1, squares, products)
    send_vecs()
    square, product = wait_parts(0)
    scale = lax.rsqrt(square + EPSILON)
    factor = scale * scale * (1.0 / dim)
    scale = scale * lax.rsqrt(square * scale * scale + EPSILON)
    energy = product * scale * scale
    squares = step(energy, scale)
    split_t()
    local_products(True)
    for b in range(nb):
        bound_v[b] = bound_v[b] * factor
    bound_out = pltpu.make_async_copy(bound_v, bound_hbm.at[0], out_sem.at[0])
    bound_out.start()
    wait_vecs()
    wait_blocks(1)
    step_slots(1, energy, scale)

    products = hopping(nothing)
    send_parts(1, squares, products)
    square, product = wait_parts(1)
    scale = lax.rsqrt(square + EPSILON)
    energy = product * scale * scale
    squares = step(energy, scale)
    send_parts(0, squares, jnp.zeros((8, dim), F32))
    which = lax.broadcasted_iota(jnp.int32, (1, 2), 1)
    energy_ref[...] = jnp.where(which == 0, first_energy, energy)
    square, _ = wait_parts(0)
    scale = lax.rsqrt(square + EPSILON)
    for b in range(nb):
        t_v[b] = t_v[b] * scale
    wave_out = pltpu.make_async_copy(t_v, wave_hbm.at[0], out_sem.at[1])
    wave_out.start()
    bound_out.wait()
    wave_out.wait()


def finish(wave, bound, energy, wave_hbm, bound_hbm, energy_hbm, sems):
    copies = [
        pltpu.make_async_copy(src, dst, sems.at[i])
        for i, (src, dst) in enumerate([(wave, wave_hbm), (bound, bound_hbm), (energy, energy_hbm)])
    ]
    for copy in copies:
        copy.start()
    for copy in copies:
        copy.wait()


def on_device(n, segs, *args):
    amplitudes, left_env, right_env, hop_left, hop_right, charges, dims, kept, fetch, slots = args
    nb, dim = amplitudes.shape[1], amplitudes.shape[2]
    nhop = hop_left.shape[2]
    cap = fetch.shape[2]
    any_space = pl.BlockSpec(memory_space=pl.ANY)
    hbm = pl.BlockSpec(memory_space=pltpu.HBM)
    smem = pl.BlockSpec(memory_space=pltpu.SMEM)
    vmem = pl.BlockSpec(memory_space=pltpu.VMEM)
    blocks = (nb, dim, dim)
    dma = pltpu.SemaphoreType.DMA
    scratch = [
        pltpu.VMEM(blocks, F32),
        pltpu.VMEM(blocks, F32),
        pltpu.VMEM(blocks, F32),
        pltpu.VMEM((nb, nhop, dim, dim), BF16),
        pltpu.VMEM((nb, nhop, dim, dim), BF16),
        pltpu.VMEM(blocks, BF16),
        pltpu.VMEM(((n - 1) * cap, dim, dim), BF16),
        pltpu.VMEM((2, n * cap, dim, dim), BF16),
        pltpu.VMEM((nb, dim, 3 * dim), BF16),
        pltpu.VMEM((nb, 3 * dim, dim), BF16),
        pltpu.VMEM((nb, 3 * dim, dim), BF16),
        pltpu.VMEM((nb, dim, 3 * dim), BF16),
        pltpu.VMEM((nb, dim, nhop * dim), BF16),
        pltpu.VMEM(blocks, F32),
        pltpu.VMEM(blocks, F32),
        pltpu.VMEM(blocks, F32),
        pltpu.VMEM((2, n, 16, dim), F32),
        pltpu.VMEM(blocks, BF16),
        pltpu.VMEM(blocks, BF16),
        pltpu.VMEM(blocks, F32),
        pltpu.VMEM(blocks, F32),
        pltpu.VMEM((n * cap, dim, dim), F32),
        pltpu.VMEM((n * cap, dim, dim), BF16),
        pltpu.VMEM((n * cap, dim, dim), F32),
        pltpu.VMEM((nb, 8, dim), F32),
        pltpu.VMEM(((n - 1) * cap, 8, dim), F32),
        pltpu.VMEM((n * cap, 8, dim), F32),
        pltpu.VMEM((8, dim), F32),
        pltpu.VMEM((n, 8, dim), F32),
        dma((5,)),
        dma((2, n - 1)),
        dma((2, n - 1)),
        dma((2, n - 1)),
        dma((2, n - 1)),
        dma,
        dma,
        dma((2,)),
        dma((n - 1,)),
        dma((n - 1,)),
        dma((n,)),
        dma((n,)),
    ]
    results = pl.pallas_call(
        functools.partial(kernel, n, segs, nb, dim, nhop, cap),
        out_shape=(
            jax.ShapeDtypeStruct(amplitudes.shape, F32),
            jax.ShapeDtypeStruct(amplitudes.shape, F32),
            jax.ShapeDtypeStruct((1, 2), F32),
        ),
        in_specs=[hbm] * 5 + [smem] * 5,
        out_specs=(any_space, any_space, vmem),
        scratch_shapes=scratch,
        compiler_params=pltpu.CompilerParams(
            collective_id=0, has_side_effects=True, vmem_limit_bytes=60 * 1024 * 1024
        ),
    )(
        amplitudes, left_env, right_env, hop_left, hop_right,
        charges.T, dims.T, kept, fetch.transpose(0, 2, 1), slots,
    )
    return pl.pallas_call(
        finish,
        out_shape=[jax.ShapeDtypeStruct(r.shape, r.dtype) for r in results],
        in_specs=[any_space] * 3,
        out_specs=[any_space] * 3,
        scratch_shapes=[dma((3,))],
    )(*results)


def solution(mesh):
    placed = (
        P(("job", "seg"), "blk", None, None),
        P(("job", "seg"), "blk", None, None),
        P(("job", "seg"), "blk", None, None),
        P(("job", "seg"), "blk", None, None, None),
        P(("job", "seg"), "blk", None, None, None),
        P("job", None),
        P(("job", "blk"), None),
        P(("job", "blk")),
        P("job", None, None),
        P(("job", "blk"), None),
    )
    return jax.shard_map(
        functools.partial(on_device, mesh.shape["blk"], mesh.shape["seg"]),
        mesh=mesh,
        in_specs=placed,
        out_specs=(
            P(("job", "seg"), "blk", None, None),
            P(("job", "seg"), "blk", None, None),
            P(("job", "seg"), None),
        ),
        check_vma=False,
    )
```

```python
import functools

import jax
import jax.numpy as jnp
from jax import lax
from jax.experimental import pallas as pl
from jax.experimental.pallas import tpu as pltpu
from jax.sharding import PartitionSpec as P

ITERS = 2
STEP_SIZE = 0.5
ZEEMAN = 0.5
EPSILON = 1e-06
MESH = pl.DeviceIdType.MESH
F32 = jnp.float32
BF16 = jnp.bfloat16


def mm(a, b):
    return jnp.dot(a, b, preferred_element_type=F32)


def tile_sum(values):
    rows, cols = values.shape
    return jnp.sum(values.reshape(rows // 8, 8, cols), axis=0)


def split(values):
    high = values.astype(BF16)
    return high, (values - high.astype(F32)).astype(BF16)


def each(count, body):
    if count <= 16:
        for index in range(count):
            body(index)
    else:
        lax.fori_loop(0, count, lambda index, _: (body(index), 0)[1], 0)


def kernel(
    n, segs, nb, dim, nhop, cap,
    amp_hbm, left_hbm, right_hbm, hopl_hbm, hopr_hbm,
    charges, dims, kept, fetch, slots,
    wave_hbm, bound_hbm, energy_ref,
    t_v, left_v, right_v, hopl_v, hopr_v,
    signed, send, recv, lmat, rmat, tcol, trow, inner, local, diag_v, mask_v,
    parts, inc_v, inc_send, bound_v,
    copy_v, slot_t, slot_x, slot_diag, vec_v, vec_send, vec_recv, norm_send, norm_recv,
    in_sem, send_sem, recv_sem, psend_sem, precv_sem, isend_sem, irecv_sem, out_sem,
    vsend_sem, vrecv_sem, nsend_sem, nrecv_sem,
):
    me = lax.axis_index("blk")
    seg = lax.axis_index("seg")
    seg_next = lax.rem(seg + 1, segs)
    seg_prev = lax.rem(seg + segs - 1, segs)
    peers = [lax.rem(me + d, n) for d in range(1, n)]
    group = [lax.rem(me + d, n) for d in range(n)]
    order = sorted(range(n - 1), key=lambda i: min(i + 1, n - 1 - i))
    entries = float(n * nb * dim * dim)

    loads = [
        pltpu.make_async_copy(src.at[0], dst, in_sem.at[i])
        for i, (src, dst) in enumerate(
            [(amp_hbm, t_v), (left_hbm, left_v), (right_hbm, right_v), (hopl_hbm, hopl_v), (hopr_hbm, hopr_v)]
        )
    ]
    for load in loads:
        load.start()

    barrier = pltpu.get_barrier_semaphore()
    for peer in peers:
        pl.semaphore_signal(barrier, inc=1, device_id={"blk": peer}, device_id_type=MESH)
    for peer in group:
        for other in (seg_next, seg_prev):
            pl.semaphore_signal(barrier, inc=1, device_id={"seg": other, "blk": peer}, device_id_type=MESH)

    row_at = lax.broadcasted_iota(jnp.int32, (dim, dim), 0)
    col_at = lax.broadcasted_iota(jnp.int32, (dim, dim), 1)
    signs = [(1 - 2 * (charges[0, me * nb + b] & 1)).astype(F32) for b in range(nb)]
    fields = [ZEEMAN * charges[1, me * nb + b].astype(F32) for b in range(nb)]

    def block_copy(half, i):
        return pltpu.make_async_remote_copy(
            src_ref=send.at[pl.ds(i * cap, cap)],
            dst_ref=recv.at[half, pl.ds(me * cap, cap)],
            send_sem=send_sem.at[half, i],
            recv_sem=recv_sem.at[half, i],
            device_id={"blk": peers[i]},
            device_id_type=MESH,
        )

    def part_copy(turn, i):
        return pltpu.make_async_remote_copy(
            src_ref=parts.at[turn, me],
            dst_ref=parts.at[turn, me],
            send_sem=psend_sem.at[turn, i],
            recv_sem=precv_sem.at[turn, i],
            device_id={"blk": peers[i]},
            device_id_type=MESH,
        )

    def vec_copy(i):
        return pltpu.make_async_remote_copy(
            src_ref=vec_send.at[pl.ds(i * cap, cap)],
            dst_ref=vec_recv.at[pl.ds(me * cap, cap)],
            send_sem=vsend_sem.at[i],
            recv_sem=vrecv_sem.at[i],
            device_id={"blk": peers[i]},
            device_id_type=MESH,
        )

    def norm_copy(i):
        return pltpu.make_async_remote_copy(
            src_ref=norm_send,
            dst_ref=norm_recv.at[me],
            send_sem=nsend_sem.at[i],
            recv_sem=nrecv_sem.at[i],
            device_id={"blk": group[i], "seg": seg_next},
            device_id_type=MESH,
        )

    def picked(device, c):
        return jnp.maximum(fetch[device, c, me], 0)

    def send_blocks(half):
        for i in order:
            for c in range(cap):
                send[i * cap + c] = signed[picked(peers[i], c)]
            block_copy(half, i).start()
        for c in range(cap):
            recv[half, me * cap + c] = signed[picked(me, c)]

    def wait_blocks(half):
        for i in range(n - 1):
            block_copy(half, i).wait()

    def diag_row(value):
        return jnp.sum(jnp.where(row_at == col_at, value, 0.0), axis=0, keepdims=True)

    def diag_of(pair):
        column = jnp.sum(jnp.where(row_at == col_at, pair[0:1], 0.0), axis=1, keepdims=True)
        return column + pair[1:2]

    def send_vecs():
        for i in order:
            for c in range(cap):
                vec_send[i * cap + c] = vec_v[picked(peers[i], c)]
            vec_copy(i).start()
        for c in range(cap):
            vec_recv[me * cap + c] = vec_v[picked(me, c)]

    def wait_vecs():
        for i in range(n - 1):
            vec_copy(i).wait()

        def one(index):
            slot_diag[index] = diag_of(vec_recv[index])

        each(n * cap, one)

    def send_parts(turn, squares, products):
        parts[turn, me] = jnp.concatenate([squares, products], axis=0)
        for i in order:
            part_copy(turn, i).start()

    def total_of(tile):
        return jnp.sum(tile, axis=(0, 1), keepdims=True)

    def wait_parts(turn):
        for i in range(n - 1):
            part_copy(turn, i).wait()
        total = parts[turn, 0]
        for i in range(1, n):
            total = total + parts[turn, i]
        return total_of(total[0:8]) / entries, total_of(total[8:16]) / entries

    def split_t():
        for b in range(nb):
            high, low = split(t_v[b])
            tcol[b, 0:dim] = high
            tcol[b, dim:2 * dim] = high
            tcol[b, 2 * dim:3 * dim] = low
            trow[b, :, 0:dim] = high
            trow[b, :, dim:2 * dim] = high
            trow[b, :, 2 * dim:3 * dim] = low

    def set_left(b, value):
        high, low = split(value)
        lmat[b, :, 0:dim] = high
        lmat[b, :, dim:2 * dim] = low
        lmat[b, :, 2 * dim:3 * dim] = high

    def local_products(with_left):
        for b in range(nb):
            value = mm(trow[b], rmat[b]) + fields[b] * t_v[b]
            if with_left:
                value = value + mm(lmat[b], tcol[b])
            local[b] = value

    def hopping(finish):
        for b in range(nb):
            for k in range(nhop):
                inner[b, :, k * dim:(k + 1) * dim] = mm(hopl_v[b, k], slot_x[slots[b, k]]).astype(BF16)
            local[b] = local[b] + mm(inner[b], hopr_v[b].reshape(nhop * dim, dim))
        finish()
        products = jnp.zeros((8, dim), F32)
        for b in range(nb):
            image = mask_v[b] * local[b]
            local[b] = image
            products = products + tile_sum(t_v[b] * image)
        return products

    def send_image(half, squares, products):
        guess = total_of(products) / (total_of(squares) + 1e-30)
        for b in range(nb):
            behind = signs[b] * t_v[b] - copy_v[b]
            weight = guess + (1.0 / STEP_SIZE) * (1.0 + jnp.abs(diag_v[b] - guess))
            signed[b] = (signs[b] * local[b] - behind * weight).astype(BF16)
        send_blocks(half)

    def advance(old, image, diag, energy, scale):
        change = (image - energy * old) / (1.0 + jnp.abs(diag - energy))
        return scale * (old - STEP_SIZE * change)

    def step(energy, scale):
        squares = jnp.zeros((8, dim), F32)
        for b in range(nb):
            new = advance(t_v[b], local[b], diag_v[b], energy, scale)
            t_v[b] = new
            squares = squares + tile_sum(new * new)
        return squares

    def step_copies(energy, scale):
        for b in range(nb):
            copy_v[b] = advance(copy_v[b], signed[b].astype(F32), diag_v[b], energy, scale)

    def step_slots(half, energy, scale):
        def one(index):
            new = advance(slot_t[index], recv[half, index].astype(F32), slot_diag[index], energy, scale)
            slot_t[index] = new
            slot_x[index] = new.astype(BF16)

        each(n * cap, one)

    def nothing():
        pass

    squares = jnp.zeros((8, dim), F32)
    loads[0].wait()
    for b in range(nb):
        live = jnp.where((row_at < dims[0, b]) & (col_at < dims[1, b]), 1.0, 0.0)
        mask_v[b] = live
        new = live * t_v[b]
        t_v[b] = new
        first = (new * signs[b]).astype(BF16)
        signed[b] = first
        copy_v[b] = first.astype(F32)
        squares = squares + tile_sum(new * new)
    pl.semaphore_wait(barrier, n - 1 + 2 * n)
    send_blocks(0)
    loads[1].wait()
    loads[2].wait()
    for b in range(nb):
        vec_v[b, 0:1] = diag_row(left_v[b]) + fields[b]
        vec_v[b, 1:2] = diag_row(right_v[b])
    send_vecs()
    split_t()
    for b in range(nb):
        set_left(b, left_v[b])
        high, low = split(right_v[b])
        rmat[b, 0:dim] = high
        rmat[b, dim:2 * dim] = low
        rmat[b, 2 * dim:3 * dim] = high
        diag_v[b] = diag_of(vec_v[b])
    local_products(True)
    loads[3].wait()
    loads[4].wait()
    wait_blocks(0)

    def widen(index):
        first = recv[0, index]
        slot_x[index] = first
        slot_t[index] = first.astype(F32)

    each(n * cap, widen)

    products = hopping(nothing)
    send_parts(0, squares, products)
    send_image(1, squares, products)
    wait_vecs()
    square, product = wait_parts(0)
    scale = lax.rsqrt(square + EPSILON)
    energy = product * scale * scale
    squares = step(energy, scale)
    step_copies(energy, scale)
    split_t()
    local_products(True)
    wait_blocks(1)
    step_slots(1, energy, scale)

    products = hopping(nothing)
    send_parts(1, squares, products)
    send_image(0, squares, products)
    square, product = wait_parts(1)
    scale = lax.rsqrt(square + EPSILON)
    energy = product * scale * scale
    first_energy = energy
    squares = step(energy, scale)
    norm_send[...] = squares
    for i in range(n):
        norm_copy(i).start()
    split_t()
    for b in range(nb):
        high, low = split(mm(lmat[b], tcol[b]))
        raw = lax.dot_general(
            tcol[b],
            jnp.concatenate([high, low, high], axis=0),
            (((0,), (0,)), ((), ())),
            preferred_element_type=F32,
        )
        keep = (row_at < kept[b]) & (col_at < kept[b])
        raw = jnp.where(keep, raw, 0.0)
        bound_v[b] = raw
        inc_send[b] = raw.astype(BF16)
    inc_copy = pltpu.make_async_remote_copy(
        src_ref=inc_send,
        dst_ref=inc_v,
        send_sem=isend_sem,
        recv_sem=irecv_sem,
        device_id={"seg": seg_next},
        device_id_type=MESH,
    )
    inc_copy.start()
    step_copies(energy, scale)
    local_products(False)
    wait_blocks(0)
    step_slots(0, energy, scale)

    def add_left():
        for i in range(n):
            norm_copy(i).wait()
        total = norm_recv[0]
        for i in range(1, n):
            total = total + norm_recv[i]
        factor = (1.0 / dim) / (total_of(total) / entries + EPSILON)
        factor = jnp.where(seg > 0, factor, 0.0)
        inc_copy.wait()
        for b in range(nb):
            wide = inc_v[b].astype(F32) * factor
            set_left(b, left_v[b] + wide)
            local[b] = local[b] + mm(lmat[b], tcol[b])
            vec_v[b, 0:1] = vec_v[b, 0:1] + diag_row(wide)
            diag_v[b] = diag_of(vec_v[b])

    products = hopping(add_left)
    send_parts(0, squares, products)
    send_image(1, squares, products)
    send_vecs()
    square, product = wait_parts(0)
    scale = lax.rsqrt(square + EPSILON)
    factor = scale * scale * (1.0 / dim)
    scale = scale * lax.rsqrt(square * scale * scale + EPSILON)
    energy = product * scale * scale
    squares = step(energy, scale)
    split_t()
    local_products(True)
    for b in range(nb):
        bound_v[b] = bound_v[b] * factor
    bound_out = pltpu.make_async_copy(bound_v, bound_hbm.at[0], out_sem.at[0])
    bound_out.start()
    wait_vecs()
    wait_blocks(1)
    step_slots(1, energy, scale)

    products = hopping(nothing)
    send_parts(1, squares, products)
    square, product = wait_parts(1)
    scale = lax.rsqrt(square + EPSILON)
    energy = product * scale * scale
    squares = step(energy, scale)
    send_parts(0, squares, jnp.zeros((8, dim), F32))
    which = lax.broadcasted_iota(jnp.int32, (1, 2), 1)
    energy_ref[...] = jnp.where(which == 0, first_energy, energy)
    square, _ = wait_parts(0)
    scale = lax.rsqrt(square + EPSILON)
    for b in range(nb):
        t_v[b] = t_v[b] * scale
    wave_out = pltpu.make_async_copy(t_v, wave_hbm.at[0], out_sem.at[1])
    wave_out.start()
    bound_out.wait()
    wave_out.wait()


def finish(wave, bound, energy, wave_out, bound_out, energy_out):
    wave_out[...] = wave[...]
    bound_out[...] = bound[...]
    energy_out[...] = energy[...]


def on_device(n, segs, *args):
    amplitudes, left_env, right_env, hop_left, hop_right, charges, dims, kept, fetch, slots = args
    nb, dim = amplitudes.shape[1], amplitudes.shape[2]
    nhop = hop_left.shape[2]
    cap = fetch.shape[2]
    any_space = pl.BlockSpec(memory_space=pl.ANY)
    hbm = pl.BlockSpec(memory_space=pltpu.HBM)
    smem = pl.BlockSpec(memory_space=pltpu.SMEM)
    vmem = pl.BlockSpec(memory_space=pltpu.VMEM)
    blocks = (nb, dim, dim)
    dma = pltpu.SemaphoreType.DMA
    scratch = [
        pltpu.VMEM(blocks, F32),
        pltpu.VMEM(blocks, F32),
        pltpu.VMEM(blocks, F32),
        pltpu.VMEM((nb, nhop, dim, dim), BF16),
        pltpu.VMEM((nb, nhop, dim, dim), BF16),
        pltpu.VMEM(blocks, BF16),
        pltpu.VMEM(((n - 1) * cap, dim, dim), BF16),
        pltpu.VMEM((2, n * cap, dim, dim), BF16),
        pltpu.VMEM((nb, dim, 3 * dim), BF16),
        pltpu.VMEM((nb, 3 * dim, dim), BF16),
        pltpu.VMEM((nb, 3 * dim, dim), BF16),
        pltpu.VMEM((nb, dim, 3 * dim), BF16),
        pltpu.VMEM((nb, dim, nhop * dim), BF16),
        pltpu.VMEM(blocks, F32),
        pltpu.VMEM(blocks, F32),
        pltpu.VMEM(blocks, F32),
        pltpu.VMEM((2, n, 16, dim), F32),
        pltpu.VMEM(blocks, BF16),
        pltpu.VMEM(blocks, BF16),
        pltpu.VMEM(blocks, F32),
        pltpu.VMEM(blocks, F32),
        pltpu.VMEM((n * cap, dim, dim), F32),
        pltpu.VMEM((n * cap, dim, dim), BF16),
        pltpu.VMEM((n * cap, dim, dim), F32),
        pltpu.VMEM((nb, 8, dim), F32),
        pltpu.VMEM(((n - 1) * cap, 8, dim), F32),
        pltpu.VMEM((n * cap, 8, dim), F32),
        pltpu.VMEM((8, dim), F32),
        pltpu.VMEM((n, 8, dim), F32),
        dma((5,)),
        dma((2, n - 1)),
        dma((2, n - 1)),
        dma((2, n - 1)),
        dma((2, n - 1)),
        dma,
        dma,
        dma((2,)),
        dma((n - 1,)),
        dma((n - 1,)),
        dma((n,)),
        dma((n,)),
    ]
    results = pl.pallas_call(
        functools.partial(kernel, n, segs, nb, dim, nhop, cap),
        out_shape=(
            jax.ShapeDtypeStruct(amplitudes.shape, F32),
            jax.ShapeDtypeStruct(amplitudes.shape, F32),
            jax.ShapeDtypeStruct((1, 2), F32),
        ),
        in_specs=[hbm] * 5 + [smem] * 5,
        out_specs=(any_space, any_space, vmem),
        scratch_shapes=scratch,
        compiler_params=pltpu.CompilerParams(
            collective_id=0, has_side_effects=True, vmem_limit_bytes=60 * 1024 * 1024
        ),
    )(
        amplitudes, left_env, right_env, hop_left, hop_right,
        charges.T, dims.T, kept, fetch.transpose(0, 2, 1), slots,
    )
    return pl.pallas_call(
        finish,
        out_shape=[jax.ShapeDtypeStruct(r.shape, r.dtype) for r in results],
        in_specs=[vmem] * 3,
        out_specs=[vmem] * 3,
    )(*results)


def solution(mesh):
    placed = (
        P(("job", "seg"), "blk", None, None),
        P(("job", "seg"), "blk", None, None),
        P(("job", "seg"), "blk", None, None),
        P(("job", "seg"), "blk", None, None, None),
        P(("job", "seg"), "blk", None, None, None),
        P("job", None),
        P(("job", "blk"), None),
        P(("job", "blk")),
        P("job", None, None),
        P(("job", "blk"), None),
    )
    return jax.shard_map(
        functools.partial(on_device, mesh.shape["blk"], mesh.shape["seg"]),
        mesh=mesh,
        in_specs=placed,
        out_specs=(
            P(("job", "seg"), "blk", None, None),
            P(("job", "seg"), "blk", None, None),
            P(("job", "seg"), None),
        ),
        check_vma=False,
    )
```
